256 devices in a mesh: dp: 16 (over y_hi, z), mp: 16 (over y_lo, x, core).
Axes of the slice: x: 4, y: 4 (y_hi: 2, y_lo: 2; y = y_hi * 2 + y_lo), z: 8, core: 2. Of those that a mesh axis runs over, the one named last changes fastest.
Arguments:
- tokens: bfloat16 [32, 128, 6144], P('dp', 'mp'), may hold values from -6 to 6
- segment_ids: int32 [32, 128], P('dp'), may hold values from 0 to 3, never falling along the last dimension, each value on 1 to 64 neighbouring positions
- block_order: int32 [32], replicated, may hold values from 0 to 31, each once
- layer_norm_gain: float32 [6144], replicated, may hold values from 0.25 to 1.75
- w_proj: bfloat16 [6144, 3, 4096], P(None, None, 'mp'), as said below
- d_attended: bfloat16 [4096, 4096], P('dp', 'mp'), may hold values from -6 to 6
Outputs:
- attended: bfloat16 [4096, 4096], P('dp', 'mp')
- token_block_gradient: bfloat16 [32, 128, 6144], P('dp', 'mp')
- d_proj: bfloat16 [6144, 3, 4096], P('dp', None, 'mp')
- norm_gain_gradient: float32 [6144], replicated
The draws below stay inside these ranges and needn't reach their ends.
Inputs may be any that keep to these rules, and one draw needn't show every extreme that they name: `segment_ids`: within each block the ids never fall and number its images from 0. `block_order`: each block number appears once. `w_proj`: entries are at most 6 / sqrt(6144) in magnitude.
All inputs are finite; a program needn't handle non-finite values.
Results may differ from the reference program's by a relative error of at most 0.025.
The reference program's roundings to bfloat16 on the way count: a program that leaves them out, or rounds other values in their place, can miss the bound.
Values may be sent and summed in bfloat16 or wider, within the bound.
A program may use at most 128 MiB of HBM per device.

```python
import math
import jax
import jax.numpy as jnp
import numpy as np
from jax import lax

D = 6144
HEADS = 32
HD = 128
BLK = 128
BG = 2
NB = 32
TOKENS = 4096
N_DP = 16
N_MP = 16


def draw_tokens(key, part):
    key = jax.random.fold_in(key, 11)
    rows = jax.random.truncated_normal(key, -6.0, 6.0, (NB, BLK, D), jnp.float32)
    return rows.astype(jnp.bfloat16)


def draw_w_proj(key, part):
    key = jax.random.fold_in(key, 23)
    weights = jax.random.truncated_normal(key, -6.0, 6.0, (D, 3, HEADS * HD), jnp.float32) * D ** (-0.5)
    return weights.astype(jnp.bfloat16)


def level_of(stream_key, extent, shards, low, top_value):
    loudness, own = 1.0, jax.random.fold_in(stream_key, 6)
    for axis_at, shards_of in shards:
        draws = jnp.exp(jax.random.uniform(jax.random.fold_in(own, axis_at), (shards_of,), jnp.float32, low / len(shards), top_value / len(shards)))
        loudness = loudness * jnp.repeat(draws, extent[axis_at] // shards_of).reshape([-1 if axis == axis_at else 1 for axis in range(len(extent))])
    return loudness


def split_up(amount, total, most, skew):
    portions = [(1 << 20) // math.isqrt(grade ** skew) + 1 for grade in range(2, amount + 1)]
    rest, given = total - most - (amount - 1), [1] * (amount - 1)
    while rest > 0:
        movable = [i for i in range(amount - 1) if given[i] < most]
        pool, remaining = sum([portions[i] for i in movable]), rest
        for i in movable:
            more = min(most - given[i], max(1, remaining * portions[i] // pool), rest)
            given[i] = given[i] + more
            rest = rest - more
    return np.array([most] + given)


def uneven_parts(stream_key, number_of, total, most, lean):
    if number_of == 2:
        one = jax.random.randint(stream_key, (), max(1, total - most), min(most, total - 1) + 1)
        return jnp.stack([one, total - one])
    sizes = jnp.asarray(split_up(number_of, total, most, lean), jnp.int32)
    couples = (number_of - 1) // 2
    giver, taker = sizes[1:1 + 2 * couples:2], sizes[2:2 + 2 * couples:2]
    slack = jnp.minimum(giver - 1, most - taker)
    shifted = jax.random.randint(jax.random.fold_in(stream_key, 1), (couples,), 0, 1 << 20) % (slack + 1)
    sizes = sizes.at[1:1 + 2 * couples:2].set(giver - shifted).at[2:2 + 2 * couples:2].set(taker + shifted)
    return sizes[jax.random.permutation(jax.random.fold_in(stream_key, 2), number_of)]


def centred(stream_key, shape, scale, bound, shards=(), held_as=jnp.bfloat16):
    entries = scale * jax.random.normal(stream_key, shape, jnp.float32)
    if shards:
        entries = entries * level_of(stream_key, shape, shards, -0.22, 0.18)
    return jnp.clip(entries, -bound, bound).astype(held_as)


def setup_inputs(seed: int = 0) -> dict:
    splits = jax.random.split(jax.random.key(seed), 7)
    return {
        "tokens": draw_tokens(jax.random.fold_in(splits[6], 71), 0),
        "segment_ids": jax.vmap(lambda own: jnp.searchsorted(jnp.cumsum(uneven_parts(own, 4, BLK, BLK // 2, 1)), jnp.arange(BLK), side="right"))(jax.random.split(splits[1], NB)).reshape((NB, BLK)).astype(jnp.int32),
        "block_order": jax.random.permutation(splits[2], NB).astype(jnp.int32),
        "layer_norm_gain": jnp.clip(1.0 + 0.15 * jax.random.normal(splits[3], (D,), jnp.float32), 0.25, 1.75),
        "w_proj": draw_w_proj(jax.random.fold_in(splits[6], 71), 0),
        "d_attended": centred(splits[5], (TOKENS, HEADS * HD), 1.0, 6.0, ((0, 16), (1, 16))),
    }


def layer_statistics(rows):
    center = rows - lax.optimization_barrier(jnp.mean(rows, axis=-1, keepdims=True))
    inverse_deviation = lax.rsqrt(lax.optimization_barrier(jnp.mean(center * center, axis=-1, keepdims=True)) + 1e-06)
    return (center * inverse_deviation, inverse_deviation)

def attend_forward(query, keys, values, segs):
    scale = HD ** (-0.5)
    scores = jnp.einsum('bqhd,bkhd->bhqk', query.astype(jnp.float32), keys.astype(jnp.float32)) * scale
    same = (segs[:, :, None] == segs[:, None, :])[:, None]
    scores = jnp.where(same, scores, -1e+30)
    peak = lax.optimization_barrier(jnp.max(scores, axis=-1, keepdims=True))
    expo = jnp.exp(scores - peak)
    probs = expo / lax.optimization_barrier(jnp.sum(expo, axis=-1, keepdims=True))
    probs_b = probs.astype(jnp.bfloat16)
    out = jnp.einsum('bhqk,bkhd->bqhd', probs_b.astype(jnp.float32), values.astype(jnp.float32))
    return (out.astype(jnp.bfloat16), probs, probs_b)

def attend_backward(query, keys, values, probs, probs_b, grad_out):
    scale = HD ** (-0.5)
    grad32 = grad_out.astype(jnp.float32)
    dprob = jnp.einsum('bqhd,bkhd->bhqk', grad32, values.astype(jnp.float32))
    dvalue = jnp.einsum('bhqk,bqhd->bkhd', probs_b.astype(jnp.float32), grad32)
    delta = lax.optimization_barrier(jnp.sum(probs * dprob, axis=-1, keepdims=True))
    dscore = (probs * (dprob - delta)).astype(jnp.bfloat16).astype(jnp.float32)
    dquery = jnp.einsum('bhqk,bkhd->bqhd', dscore, keys.astype(jnp.float32)) * scale
    dkey = jnp.einsum('bhqk,bqhd->bkhd', dscore, query.astype(jnp.float32)) * scale
    return jnp.stack([dquery, dkey, dvalue], axis=2).astype(jnp.bfloat16)

def reference(tokens, segment_ids, block_order, layer_norm_gain, w_proj, d_attended):
    relocated_blocks = tokens[block_order]
    segs = segment_ids[block_order]
    centered_input, inverse_deviation = layer_statistics(relocated_blocks.astype(jnp.float32))
    normalized_input = (centered_input * layer_norm_gain).astype(jnp.bfloat16)
    proj = jnp.einsum('btd,dcf->btcf', normalized_input.astype(jnp.float32), w_proj.astype(jnp.float32)).astype(jnp.bfloat16)
    nblk, blen = (proj.shape[0], proj.shape[1])
    heads = proj.shape[3] // HD
    split = proj.reshape(nblk, blen, 3, heads, HD)
    query, keys, values = (split[:, :, 0], split[:, :, 1], split[:, :, 2])
    out, probs, probs_b = attend_forward(query, keys, values, segs)
    attended = out.reshape(nblk * blen, heads * HD)
    grad_out = d_attended.reshape(nblk, blen, heads, HD)
    dqkv = attend_backward(query, keys, values, probs, probs_b, grad_out).reshape(nblk, blen, 3, heads * HD)
    width = heads * HD
    d_proj = jnp.zeros((normalized_input.shape[2], 3, width), jnp.float32)
    for group in range(N_DP):
        rows = slice(group * BG, (group + 1) * BG)
        term = jnp.einsum('btd,btcf->dcf', normalized_input[rows].astype(jnp.float32), dqkv[rows].astype(jnp.float32))
        d_proj = d_proj + term.astype(jnp.bfloat16).astype(jnp.float32)
    run = width // N_MP
    normalized_gradient = jnp.zeros(normalized_input.shape, jnp.float32)
    for shard in range(N_MP):
        cols = slice(shard * run, (shard + 1) * run)
        term = jnp.einsum('btcf,dcf->btd', dqkv[:, :, :, cols].astype(jnp.float32), w_proj[:, :, cols].astype(jnp.float32))
        normalized_gradient = normalized_gradient + term.astype(jnp.bfloat16).astype(jnp.float32)
    norm_gain_gradient = lax.optimization_barrier(jnp.sum(normalized_gradient * centered_input, axis=(0, 1)))
    gain_scaled = normalized_gradient * layer_norm_gain
    token_block_gradient = inverse_deviation * (gain_scaled - lax.optimization_barrier(jnp.mean(gain_scaled, axis=-1, keepdims=True)) - centered_input * lax.optimization_barrier(jnp.mean(gain_scaled * centered_input, axis=-1, keepdims=True)))
    return (attended, token_block_gradient.astype(jnp.bfloat16), d_proj.astype(jnp.bfloat16), norm_gain_gradient)
```

```python
import jax
import jax.numpy as jnp
from jax import lax
from jax.experimental import pallas as pl
from jax.experimental.pallas import tpu as pltpu
from jax.sharding import PartitionSpec as P

D = 6144
HD = 128
PC = 384
NP = 16
F32 = jnp.float32
BF16 = jnp.bfloat16
MESH = pl.DeviceIdType.MESH
ORDER = (2, 0, 1)


def dot(a, b, ca=1, cb=0):
    return lax.dot_general(a, b, (((ca,), (cb,)), ((), ())), preferred_element_type=F32)


def hops_of(way, head):
    return 4 if way == head else 3


def kernel(
    order, tok, seg, gain, w_hbm, datt,
    att_o, tbg_o, dproj_o, gg_o,
    wv, r1, r2s, r2, segp, sega, gat, nsb, xh, proj, zb, nt, dnb, rsa, b1, rsb, b2, rsc,
    acc, ysnd, rl, fin, gp, g1, g2s, g2, g3s, g3,
    wsem, lsem, r1sem, r2sem, sgsem, nasem, gasem, nssem, zsem, rasem, rbsem, rcsem, ysem,
    g1sem, g2sem, g3sem,
):
    dp = lax.axis_index("dp")
    mp = lax.axis_index("mp")
    yh, z = dp // 8, dp % 8
    yl, x, core = mp // 8, (mp // 2) % 4, mp % 2

    def mpid(a, b, c):
        return a * 8 + b * 2 + c

    def mp_of(slot):
        return mpid((slot // 4) % 2, slot % 4, slot // 8)

    sg = core * 8 + yl * 4 + x
    sib = (dp, mpid(yl, x, 1 - core))
    yn = (dp, mpid(1 - yl, x, core))
    xp = (dp, mpid(yl, (x + 1) % 4, core))
    xm = (dp, mpid(yl, (x + 3) % 4, core))
    xo = (dp, mpid(yl, (x + 2) % 4, core))
    zp = (yh * 8 + (z + 1) % 8, mp)
    zm = (yh * 8 + (z + 7) % 8, mp)
    yup_h = jnp.where(yl == 0, yh, 1 - yh)
    ydn_h = jnp.where(yl == 1, yh, 1 - yh)
    yup = (yup_h * 8 + z, mpid(1 - yl, x, core))
    ydn = (ydn_h * 8 + z, mpid(1 - yl, x, core))
    far = ((1 - yh) * 8 + z, mpid(1 - yl, x, core))

    def rc(src, dst, sems, dev):
        ss, rs = sems
        return pltpu.make_async_remote_copy(
            src_ref=src, dst_ref=dst, send_sem=ss, recv_sem=rs, device_id=dev, device_id_type=MESH
        )

    pend = []

    def send(src, dst, sems, dev):
        rc(src, dst, sems, dev).start()
        pend.append((src, dst, sems, dev))

    def got(dst, sems):
        rc(dst, dst, sems, sib).wait_recv()

    wcp = [
        pltpu.make_async_copy(
            w_hbm.at[:, pl.ds(k * 1536, 1536)], wv.at[:, pl.ds(k * 1536, 1536)], wsem.at[k]
        )
        for k in range(4)
    ]
    for cp in wcp:
        cp.start()

    barrier = pltpu.get_barrier_semaphore()

    def greet(i, _):
        pl.semaphore_signal(barrier, inc=1, device_id=((dp + i) % 16, mp), device_id_type=MESH)
        pl.semaphore_signal(
            barrier, inc=1, device_id=(dp, mp_of((sg + i) % 16)), device_id_type=MESH
        )
        return _

    lax.fori_loop(1, 16, greet, 0)
    pl.semaphore_signal(barrier, inc=1, device_id=far, device_id_type=MESH)
    segp[...] = jnp.zeros_like(segp)
    segp[0:2, :] = seg[...]
    pl.semaphore_wait(barrier, 31)

    def cols(j):
        return pl.ds(pl.multiple_of(j * PC, 128), PC)

    def r1_copy(i):
        d = (dp + i) % 16
        return rc(tok.at[:, cols(d)], r1.at[dp], (r1sem.at[0, i], r1sem.at[1, i]), (d, mp))

    def sg_copy(i):
        d = (dp + i) % 16
        return rc(segp, sega.at[dp], (sgsem.at[0, i], sgsem.at[1, i]), (d, mp))

    def r1_send(i, _):
        r1_copy(i).start()
        return _

    def sg_send(i, _):
        sg_copy(i).start()
        return _

    lax.fori_loop(1, 16, r1_send, 0)
    lax.fori_loop(1, 16, sg_send, 0)
    own = pltpu.make_async_copy(tok.at[:, cols(dp)], r1.at[dp], lsem.at[0])
    own.start()
    sega[dp] = segp[...]

    def source(i):
        s, b, r = i >> 4, (i >> 3) & 1, i & 7
        m = ((s >> 2) & 1) * 8 + (s & 3) * 2 + (s >> 3)
        return b * 128 + m * 8 + r

    ri = lax.broadcasted_iota(jnp.int32, (256, 256), 0)
    ci = lax.broadcasted_iota(jnp.int32, (256, 256), 1)
    perm = jnp.where(source(ri) == ci, 1.0, 0.0).astype(BF16)
    perm_t = jnp.where(source(ci) == ri, 1.0, 0.0).astype(BF16)
    g = dot(perm, datt[...]).astype(BF16)

    own.wait()

    def r1_wait(i, _):
        s = (dp + 16 - i) % 16
        got(r1.at[s], (r1sem.at[0, i], r1sem.at[1, i]))
        return _

    lax.fori_loop(1, 16, r1_wait, 0)

    def half_of(p):
        b = order[p]
        t = r1[b >> 1].astype(F32)
        return jnp.where((b & 1) == 1, t[8:16], t[0:8])

    def pick(d):
        return jnp.concatenate([half_of(2 * d), half_of(2 * d + 1)], axis=0).astype(BF16)

    def r2_copy(i):
        d = (dp + i) % 16
        return rc(r2s.at[d], r2.at[dp], (r2sem.at[0, i], r2sem.at[1, i]), (d, mp))

    def r2_send(i, _):
        d = (dp + i) % 16
        r2s[d] = pick(d)
        r2_copy(i).start()
        return _

    lax.fori_loop(1, 16, r2_send, 0)
    r2[dp] = pick(dp)

    def sg_wait(i, _):
        s = (dp + 16 - i) % 16
        got(sega.at[s], (sgsem.at[0, i], sgsem.at[1, i]))
        return _

    lax.fori_loop(1, 16, sg_wait, 0)

    def ids_of(p):
        b = order[p]
        t = sega[b >> 1].astype(F32)
        return jnp.where((b & 1) == 1, t[1:2], t[0:1])

    ids = jnp.concatenate([ids_of(2 * dp), ids_of(2 * dp + 1) + 4.0], axis=1)
    ids = jnp.broadcast_to(ids, (8, 256)).astype(BF16)
    id_row = dot(ids, perm_t)[0:1]
    id_col = dot(perm, ids, 1, 1)[:, 0:1]
    same = id_col == id_row

    def r2_wait(i, _):
        s = (dp + 16 - i) % 16
        got(r2.at[s], (r2sem.at[0, i], r2sem.at[1, i]))
        return _

    lax.fori_loop(1, 16, r2_wait, 0)

    rows = r2[...].astype(F32)
    mean = jnp.sum(jnp.sum(rows, axis=0), axis=-1, keepdims=True) * (1.0 / D)
    cen = rows - mean[None]
    var = jnp.sum(jnp.sum(cen * cen, axis=0), axis=-1, keepdims=True) * (1.0 / D)
    rstd = lax.rsqrt(var + 1e-06)
    xhat = cen * rstd[None]
    xh[...] = xhat
    for j in range(NP):
        gat[j, sg] = (xhat[j] * gain[j : j + 1, :]).astype(BF16)

    def gather(buf, sems):
        def at(k, slot):
            return buf.at[pl.ds(4 * k, 4), slot]

        def slot(a, b):
            return core * 8 + a * 4 + b

        def sm(k, n):
            return (sems.at[0, k, n], sems.at[1, k, n])

        def go(k, a, b, n, dev):
            ref = at(k, slot(a, b))
            send(ref, ref, sm(k, n), dev)

        def have(k, a, b, n):
            got(at(k, slot(a, b)), sm(k, n))

        x1, x2, x3 = (x + 1) % 4, (x + 2) % 4, (x + 3) % 4

        def stage1(k):
            go(k, yl, x, 0, yn)
            go(k, yl, x, 1, xp)
            go(k, yl, x, 2, xm)

        def stage2(k):
            have(k, 1 - yl, x, 0)
            go(k, 1 - yl, x, 3, xp)
            go(k, 1 - yl, x, 4, xm)

        def stage3(k):
            have(k, yl, x3, 1)
            go(k, yl, x3, 5, xp)
            have(k, 1 - yl, x1, 4)
            go(k, 1 - yl, x1, 6, xm)

        def stage4(k):
            have(k, yl, x1, 2)
            have(k, 1 - yl, x3, 3)
            have(k, yl, x2, 5)
            have(k, 1 - yl, x2, 6)
            ref = buf.at[pl.ds(4 * k, 4), pl.ds(core * 8, 8)]
            send(ref, ref, sm(k, 7), sib)

        def stage5(k):
            got(buf.at[pl.ds(4 * k, 4), pl.ds((1 - core) * 8, 8)], sm(k, 7))

        return stage1, stage2, stage3, stage4, stage5

    G1, G2, G3, G4, G5 = gather(gat, gasem)
    N1, N2, N3, N4, N5 = gather(nsb, nssem)
    for k in range(4):
        G1(k)

    def na_copy(i, o):
        t = (z + o) % 8
        return rc(
            gat.at[i * 8 + t, sg], nsb.at[i * 8 + z, sg],
            (nasem.at[0, i, o], nasem.at[1, i, o]), (yh * 8 + t, mp),
        )

    def na_send(o, _):
        na_copy(0, o).start()
        na_copy(1, o).start()
        return _

    lax.fori_loop(1, 8, na_send, 0)
    for i in range(2):
        nsb[i * 8 + z, sg] = gat[i * 8 + z, sg]

    def na_wait(o, _):
        s = (z + 8 - o) % 8
        for i in range(2):
            got(nsb.at[i * 8 + s, sg], (nasem.at[0, i, o], nasem.at[1, i, o]))
        return _

    for k in range(4):
        G2(k)
    lax.fori_loop(1, 8, na_wait, 0)
    for k in range(4):
        G3(k)
    for k in range(4):
        N1(k)
    for k in range(4):
        G4(k)
    for k in range(4):
        G5(k)
        wcp[k].wait()
        for q in range(2):
            j = 4 * k + 2 * q
            lhs = jnp.concatenate(
                [gat[j].reshape(256, PC), gat[j + 1].reshape(256, PC)], axis=1
            )
            for c in range(3):
                t = dot(lhs, wv[c, j * PC : (j + 2) * PC, :])
                proj[c] = t if j == 0 else proj[c] + t
        N2(k)

    scale = HD ** (-0.5)

    def zat(s, c, h):
        return zb.at[s, c, h]

    def z_send(way, hop, c, h):
        s = (z + (8 - hop if way == 0 else hop)) % 8
        ref = zat(s, c, h)
        send(
            ref, ref, (zsem.at[0, way, hop, c, h], zsem.at[1, way, hop, c, h]),
            zp if way == 0 else zm,
        )

    def z_have(way, hop, c, h):
        s = (z + (8 - hop if way == 0 else hop)) % 8
        got(zat(s, c, h), (zsem.at[0, way, hop - 1, c, h], zsem.at[1, way, hop - 1, c, h]))

    outs = []
    for h in range(2):
        lanes = slice(h * HD, (h + 1) * HD)
        q, k, v = [proj[c, :, lanes].astype(BF16) for c in range(3)]
        gh = g[:, lanes]
        s = jnp.where(same, dot(q, k, 1, 1) * scale, -1e30)
        e = jnp.exp(s - jnp.max(s, axis=-1, keepdims=True))
        probs = e / jnp.sum(e, axis=-1, keepdims=True)
        pb = probs.astype(BF16)

        def put(c, val):
            zb[z, c, h] = val.astype(BF16)
            z_send(0, 0, c, h)
            z_send(1, 0, c, h)

        put(2, dot(pb, gh, 0, 0))
        dprob = dot(gh, v, 1, 1)
        delta = jnp.sum(probs * dprob, axis=-1, keepdims=True)
        ds = (probs * (dprob - delta)).astype(BF16)
        put(0, dot(ds, k) * scale)
        put(1, dot(ds, q, 0, 0) * scale)
        outs.append(dot(pb, v).astype(BF16))
    att_o[...] = dot(perm_t, jnp.concatenate(outs, axis=1)).astype(BF16)

    dq = [jnp.concatenate([zb[z, c, 0], zb[z, c, 1]], axis=1) for c in range(3)]

    def dn_step(k):
        def body(j, _):
            at = pl.ds(pl.multiple_of(j * PC, 128), PC)
            t = dot(dq[0], wv[0, at, :], 1, 1)
            t = t + dot(dq[1], wv[1, at, :], 1, 1)
            t = t + dot(dq[2], wv[2, at, :], 1, 1)
            dnb[j] = t.astype(BF16).reshape(16, 16, PC)
            return _

        lax.fori_loop(4 * k, 4 * k + 4, body, 0)
        send(
            dnb.at[pl.ds(4 * k, 4), pl.ds((1 - core) * 8, 8)], rsa.at[pl.ds(4 * k, 4)],
            (rasem.at[0, k], rasem.at[1, k]), sib,
        )

    def s2(k):
        got(rsa.at[pl.ds(4 * k, 4)], (rasem.at[0, k], rasem.at[1, k]))
        for j in range(4 * k, 4 * k + 4):
            mine = dnb[j, pl.ds(core * 8, 8)].astype(F32)
            b1[j] = (mine + rsa[j].astype(F32)).astype(BF16)
        send(
            b1.at[pl.ds(4 * k, 4), pl.ds((1 - yl) * 4, 4)], rsb.at[pl.ds(4 * k, 4)],
            (rbsem.at[0, k], rbsem.at[1, k]), yn,
        )

    def s3(k):
        got(rsb.at[pl.ds(4 * k, 4)], (rbsem.at[0, k], rbsem.at[1, k]))
        for j in range(4 * k, 4 * k + 4):
            mine = b1[j, pl.ds(yl * 4, 4)].astype(F32)
            b2[j] = (mine + rsb[j].astype(F32)).astype(BF16)
        for o, dev in ((1, xp), (2, xo), (3, xm)):
            send(
                b2.at[pl.ds(4 * k, 4), (x + o) % 4], rsc.at[o - 1, pl.ds(4 * k, 4)],
                (rcsem.at[0, o, k], rcsem.at[1, o, k]), dev,
            )

    def w(hop, c):
        for way in range(2):
            for h in range(2):
                n = hops_of(way, h)
                if hop <= n:
                    z_have(way, hop, c, h)
                if hop < n:
                    z_send(way, hop, c, h)

    v_, q_, k_ = ORDER
    for k in range(4):
        N3(k)
    dn_step(0)
    dn_step(1)
    w(1, v_)
    dn_step(2)
    dn_step(3)
    w(1, q_)
    s2(0)
    s2(1)
    w(1, k_)
    s2(2)
    s2(3)
    w(2, v_)
    for k in range(4):
        N4(k)
    w(2, q_)
    s3(0)
    s3(1)
    w(2, k_)
    s3(2)
    s3(3)
    w(3, v_)
    for k in range(4):
        N5(k)

    def turn(s, _):
        for i in range(2):
            nt[s, i] = nsb[i * 8 + s].reshape(256, PC).T
        return _

    lax.fori_loop(0, 8, turn, 0)
    w(3, q_)
    w(3, k_)

    total = jnp.zeros((NP, 16, PC), F32)
    for k in range(4):
        for o in range(1, 4):
            got(rsc.at[o - 1, pl.ds(4 * k, 4)], (rcsem.at[0, o, k], rcsem.at[1, o, k]))
    xhat = xh[...]
    parts = []
    for j in range(NP):
        t = b2[j, x].astype(F32)
        for o in range(3):
            t = t + rsc[o, j].astype(F32)
        p = t * xhat[j]
        gp[j] = p[0:8] + p[8:16]
        parts.append(t * gain[j : j + 1, :])

    def g1_copy(i):
        s = (sg + i) % 16
        return rc(gp.at[s], g1.at[sg], (g1sem.at[0, i], g1sem.at[1, i]), (dp, mp_of(s)))

    def g1_send(i, _):
        g1_copy(i).start()
        return _

    lax.fori_loop(1, 16, g1_send, 0)
    g1[sg] = gp[sg]
    m1 = sum(jnp.sum(parts[j], axis=-1, keepdims=True) for j in range(NP)) * (1.0 / D)
    m2 = sum(jnp.sum(parts[j] * xhat[j], axis=-1, keepdims=True) for j in range(NP)) * (1.0 / D)
    for j in range(NP):
        t = rstd * (parts[j] - m1 - xhat[j] * m2)
        tbg_o[:, j * PC : (j + 1) * PC] = t.astype(BF16)

    def dproj(c):
        acc[c] = jnp.zeros((2, PC, 256), F32)

        def body(s, _):
            rhs = jnp.concatenate([zb[s, c, 0], zb[s, c, 1]], axis=1)
            for i in range(2):
                acc[c, i] += dot(nt[s, i], rhs)
            return _

        lax.fori_loop(0, 8, body, 0)
        ysnd[c] = acc[c, 1 - yh].astype(BF16)
        send(ysnd.at[c, pl.ds(0, 192)], rl.at[c, 0], (ysem.at[0, c, 0], ysem.at[1, c, 0]), yup)
        send(ysnd.at[c, pl.ds(192, 192)], rl.at[c, 1], (ysem.at[0, c, 1], ysem.at[1, c, 1]), ydn)

    def relay(c):
        for n, dev in ((0, yup), (1, ydn)):
            got(rl.at[c, n], (ysem.at[0, c, n], ysem.at[1, c, n]))
            send(
                rl.at[c, n], fin.at[c, pl.ds(192 * n, 192)],
                (ysem.at[0, c, 2 + n], ysem.at[1, c, 2 + n]), dev,
            )

    def finish(c):
        for n in range(2):
            got(fin.at[c, pl.ds(192 * n, 192)], (ysem.at[0, c, 2 + n], ysem.at[1, c, 2 + n]))
        dproj_o[c] = (acc[c, yh] + fin[c].astype(F32)).astype(BF16)

    w(4, v_)
    dproj(v_)

    def g1_wait(i, _):
        s = (sg + 16 - i) % 16
        got(g1.at[s], (g1sem.at[0, i], g1sem.at[1, i]))
        return _

    lax.fori_loop(1, 16, g1_wait, 0)
    t = jnp.sum(jnp.sum(g1[...], axis=0), axis=0, keepdims=True)
    g2s[...] = jnp.broadcast_to(t, (8, PC))

    def g2_copy(i):
        d = (dp + i) % 16
        return rc(g2s, g2.at[dp], (g2sem.at[0, i], g2sem.at[1, i]), (d, mp))

    def g2_send(i, _):
        g2_copy(i).start()
        return _

    lax.fori_loop(1, 16, g2_send, 0)
    g2[dp] = g2s[...]
    w(4, q_)
    dproj(q_)
    relay(v_)

    def g2_wait(i, _):
        s = (dp + 16 - i) % 16
        got(g2.at[s], (g2sem.at[0, i], g2sem.at[1, i]))
        return _

    lax.fori_loop(1, 16, g2_wait, 0)
    g3s[...] = jnp.sum(g2[...], axis=0)

    def g3_copy(i):
        s = (sg + i) % 16
        return rc(g3s, g3.at[sg], (g3sem.at[0, i], g3sem.at[1, i]), (dp, mp_of(s)))

    def g3_send(i, _):
        g3_copy(i).start()
        return _

    lax.fori_loop(1, 16, g3_send, 0)
    g3[sg] = g3s[...]
    w(4, k_)
    dproj(k_)
    relay(q_)
    finish(v_)
    relay(k_)

    def g3_wait(i, _):
        s = (sg + 16 - i) % 16
        got(g3.at[s], (g3sem.at[0, i], g3sem.at[1, i]))
        return _

    lax.fori_loop(1, 16, g3_wait, 0)
    for s in range(NP):
        gg_o[s : s + 1, :] = g3[s, 0:1, :]
    finish(q_)
    finish(k_)

    def drain(i, _):
        r1_copy(i).wait_send()
        sg_copy(i).wait_send()
        r2_copy(i).wait_send()
        g1_copy(i).wait_send()
        g2_copy(i).wait_send()
        g3_copy(i).wait_send()
        return _

    lax.fori_loop(1, 16, drain, 0)

    def drain_na(o, _):
        na_copy(0, o).wait_send()
        na_copy(1, o).wait_send()
        return _

    lax.fori_loop(1, 8, drain_na, 0)
    for item in pend:
        rc(*item).wait_send()


def per_device(tokens, segment_ids, block_order, layer_norm_gain, w_proj, d_attended):
    vm = pl.BlockSpec(memory_space=pltpu.VMEM)
    dma = pltpu.SemaphoreType.DMA
    V = pltpu.VMEM
    big = (NP, 16, 16, PC)
    att, tbg, dproj, gg = pl.pallas_call(
        kernel,
        out_shape=(
            jax.ShapeDtypeStruct((256, 256), BF16),
            jax.ShapeDtypeStruct((16, D), BF16),
            jax.ShapeDtypeStruct((3, PC, 256), BF16),
            jax.ShapeDtypeStruct((NP, PC), F32),
        ),
        in_specs=[
            pl.BlockSpec(memory_space=pltpu.SMEM), vm, vm, vm,
            pl.BlockSpec(memory_space=pl.ANY), vm,
        ],
        out_specs=(vm, vm, vm, vm),
        scratch_shapes=[
            V((3, D, 256), BF16),
            V((NP, 16, PC), BF16),
            V((NP, 16, PC), BF16),
            V((NP, 16, PC), BF16),
            V((8, 128), jnp.int32),
            V((NP, 8, 128), jnp.int32),
            V(big, BF16),
            V(big, BF16),
            V((NP, 16, PC), F32),
            V((3, 256, 256), F32),
            V((8, 3, 2, 256, HD), BF16),
            V((8, 2, PC, 256), BF16),
            V(big, BF16),
            V((NP, 8, 16, PC), BF16),
            V((NP, 8, 16, PC), BF16),
            V((NP, 4, 16, PC), BF16),
            V((NP, 4, 16, PC), BF16),
            V((3, NP, 16, PC), BF16),
            V((3, 2, PC, 256), F32),
            V((3, PC, 256), BF16),
            V((3, 2, 192, 256), BF16),
            V((3, PC, 256), BF16),
            V((NP, 8, PC), F32),
            V((NP, 8, PC), F32),
            V((8, PC), F32),
            V((NP, 8, PC), F32),
            V((8, PC), F32),
            V((NP, 8, PC), F32),
            dma((4,)),
            dma((1,)),
            dma((2, 16)),
            dma((2, 16)),
            dma((2, 16)),
            dma((2, 2, 8)),
            dma((2, 4, 8)),
            dma((2, 4, 8)),
            dma((2, 2, 4, 3, 2)),
            dma((2, 4)),
            dma((2, 4)),
            dma((2, 4, 4)),
            dma((2, 3, 4)),
            dma((2, 16)),
            dma((2, 16)),
            dma((2, 16)),
        ],
        compiler_params=pltpu.CompilerParams(
            collective_id=0, has_side_effects=True, vmem_limit_bytes=60 * 1024 * 1024
        ),
    )(
        block_order,
        tokens.reshape(16, D),
        segment_ids,
        layer_norm_gain.reshape(NP, PC),
        jnp.transpose(w_proj, (1, 0, 2)),
        d_attended,
    )
    return att, tbg.reshape(2, 8, D), jnp.transpose(dproj, (1, 0, 2)), gg.reshape(D)


def solution(mesh):
    placed = (P("dp", "mp", None), P("dp", None), P(), P(), P(None, None, "mp"), P("dp", "mp"))
    return jax.shard_map(
        per_device,
        mesh=mesh,
        in_specs=placed,
        out_specs=(P("dp", "mp"), P("dp", "mp", None), P("dp", None, "mp"), P()),
        check_vma=False,
    )
```

```python
import jax
import jax.numpy as jnp
from jax import lax
from jax.experimental import pallas as pl
from jax.experimental.pallas import tpu as pltpu
from jax.sharding import PartitionSpec as P

D = 6144
HD = 128
PC = 384
NC = 2
NP = 16
F32 = jnp.float32
BF16 = jnp.bfloat16
MESH = pl.DeviceIdType.MESH
CHUNKS = ((0, 2), (0, 0), (0, 1), (1, 2), (1, 0), (1, 1))


def dot(a, b, ca=1, cb=0):
    return lax.dot_general(a, b, (((ca,), (cb,)), ((), ())), preferred_element_type=F32)


def hops_of(way, i):
    return 4 if way == i % 2 else 3


def kernel(
    order, tok, seg, gain_ref, w_hbm, datt,
    att_o, tbg_o, dproj_o, gg_o,
    wv, r1, r2s, r2, segp, sega, gn, nrm, gat, nrow, nsb, xh, proj, zb, nt,
    dnb, rsa, b1, rsb, b2, rsc, rsx, b3, rsy,
    acc, ysnd, fin, gp, gs, ga,
    wsem, lsem, r1sem, r2sem, sgsem, nasem, gasem, nssem, zsem, rasem, rbsem, rcsem, rxsem, rysem, ysem,
    gsem,
):
    dp = lax.axis_index("dp")
    mp = lax.axis_index("mp")
    yh, z = dp // 8, dp % 8
    yl, x, core = mp // 8, (mp // 2) % 4, mp % 2

    def mpid(a, b, c):
        return a * 8 + b * 2 + c

    def mp_of(slot):
        return mpid((slot // 4) % 2, slot % 4, slot // 8)

    sg = core * 8 + yl * 4 + x
    sib = (dp, mpid(yl, x, 1 - core))
    yn = (dp, mpid(1 - yl, x, core))
    xp = (dp, mpid(yl, (x + 1) % 4, core))
    xm = (dp, mpid(yl, (x + 3) % 4, core))
    xo = (dp, mpid(yl, (x + 2) % 4, core))
    zp = (yh * 8 + (z + 1) % 8, mp)
    zm = (yh * 8 + (z + 7) % 8, mp)
    yo = ((1 - yh) * 8 + z, mp)

    def rc(src, dst, sems, dev):
        ss, rs = sems
        return pltpu.make_async_remote_copy(
            src_ref=src, dst_ref=dst, send_sem=ss, recv_sem=rs, device_id=dev, device_id_type=MESH
        )

    def far_first(t):
        half = (t % 8 + 1) // 2
        o = jnp.where(t % 2 == 1, 4 - half, 4 + half) % 8
        return (1 - t // 8) * 8 + o

    def dp_to(i):
        return jnp.where(i >= 8, 1 - yh, yh) * 8 + (z + i) % 8

    def dp_from(i):
        return jnp.where(i >= 8, 1 - yh, yh) * 8 + (z + 16 - i) % 8

    pend = []

    def send(src, dst, sems, dev):
        rc(src, dst, sems, dev).start()
        pend.append((src, dst, sems, dev))

    def got(dst, sems):
        rc(dst, dst, sems, sib).wait_recv()

    wcp = [
        pltpu.make_async_copy(
            w_hbm.at[:, pl.ds(k * 1536, 1536)], wv.at[:, pl.ds(k * 1536, 1536)], wsem.at[k]
        )
        for k in range(4)
    ]
    for cp in wcp:
        cp.start()

    barrier = pltpu.get_barrier_semaphore()

    def greet(t, _):
        pl.semaphore_signal(
            barrier, inc=1, device_id=(dp_to(far_first(t)), mp), device_id_type=MESH
        )
        pl.semaphore_signal(
            barrier, inc=1, device_id=(dp, mp_of((sg + t + 1) % 16)), device_id_type=MESH
        )
        return _

    lax.fori_loop(0, 15, greet, 0)
    segp[...] = jnp.zeros_like(segp)
    segp[0:2, :] = seg[...]
    for j in range(NP):
        gn[j : j + 1, :] = jnp.concatenate(
            [gain_ref[3 * j + n : 3 * j + n + 1, :] for n in range(3)], axis=1
        )
    pl.semaphore_wait(barrier, 30)

    def cols(j):
        return pl.ds(pl.multiple_of(j * PC, 128), PC)

    def r1_copy(i):
        d = dp_to(i)
        return rc(tok.at[:, cols(d)], r1.at[dp], (r1sem.at[0, i], r1sem.at[1, i]), (d, mp))

    def sg_copy(i):
        return rc(segp, sega.at[dp], (sgsem.at[0, i], sgsem.at[1, i]), (dp_to(i), mp))

    def r1_send(t, _):
        r1_copy(far_first(t)).start()
        return _

    lax.fori_loop(0, 15, r1_send, 0)
    own = pltpu.make_async_copy(tok.at[:, cols(dp)], r1.at[dp], lsem.at[0])
    own.start()
    sega[dp] = segp[...]

    def source(i):
        s, r = i >> 3, i & 7
        m = ((s >> 2) & 1) * 8 + (s & 3) * 2 + (s >> 3)
        return m * 8 + r

    ri = lax.broadcasted_iota(jnp.int32, (128, 128), 0)
    ci = lax.broadcasted_iota(jnp.int32, (128, 128), 1)
    perm = jnp.where(source(ri) == ci, 1.0, 0.0).astype(BF16)
    perm_t = jnp.where(source(ci) == ri, 1.0, 0.0).astype(BF16)

    own.wait()

    def r1_wait(i, _):
        got(r1.at[dp_from(i)], (r1sem.at[0, i], r1sem.at[1, i]))
        return _

    lax.fori_loop(1, 16, r1_wait, 0)

    def half_of(p):
        b = order[p]
        t = r1[b >> 1].astype(F32)
        return jnp.where((b & 1) == 1, t[8:16], t[0:8])

    def pick(d):
        return jnp.concatenate([half_of(2 * d), half_of(2 * d + 1)], axis=0).astype(BF16)

    def r2_copy(i):
        d = dp_to(i)
        return rc(r2s.at[d], r2.at[dp], (r2sem.at[0, i], r2sem.at[1, i]), (d, mp))

    def r2_send(t, _):
        i = far_first(t)
        d = dp_to(i)
        r2s[d] = pick(d)
        r2_copy(i).start()
        return _

    lax.fori_loop(0, 15, r2_send, 0)
    r2[dp] = pick(dp)

    def sg_send(i, _):
        sg_copy(i).start()
        return _

    lax.fori_loop(1, 16, sg_send, 0)

    def sg_wait(i, _):
        got(sega.at[dp_from(i)], (sgsem.at[0, i], sgsem.at[1, i]))
        return _

    def ids_of(p):
        b = order[p]
        t = sega[b >> 1].astype(F32)
        return jnp.where((b & 1) == 1, t[1:2], t[0:1])

    def same_image(b):
        ids = jnp.broadcast_to(ids_of(2 * dp + b), (8, 128)).astype(BF16)
        return dot(perm, ids, 1, 1)[:, 0:1] == dot(ids, perm_t)[0:1]

    def r2_wait(i, _):
        got(r2.at[dp_from(i)], (r2sem.at[0, i], r2sem.at[1, i]))
        return _

    lax.fori_loop(1, 16, r2_wait, 0)

    rows = r2[...].astype(F32)
    mean = jnp.sum(jnp.sum(rows, axis=0), axis=-1, keepdims=True) * (1.0 / D)
    cen = rows - mean[None]
    var = jnp.sum(jnp.sum(cen * cen, axis=0), axis=-1, keepdims=True) * (1.0 / D)
    rstd = lax.rsqrt(var + 1e-06)
    xhat = cen * rstd[None]
    normed = [xhat[j] * gn[j : j + 1, :] for j in range(NP)]
    for b in range(2):
        half = slice(8 * b, 8 * b + 8)
        for j in range(8):
            both = jnp.concatenate([normed[j][half], normed[j + 8][half]], axis=0)
            gat[8 * b + j, sg] = both.astype(BF16)

    def gather(buf, sems, chunks):
        n = NP // chunks

        def at(k, slot):
            return buf.at[pl.ds(n * k, n), slot]

        def slot(a, b):
            return core * 8 + a * 4 + b

        def sm(k, m):
            return (sems.at[0, k, m], sems.at[1, k, m])

        def go(k, a, b, m, dev):
            ref = at(k, slot(a, b))
            send(ref, ref, sm(k, m), dev)

        def have(k, a, b, m):
            got(at(k, slot(a, b)), sm(k, m))

        x1, x2, x3 = (x + 1) % 4, (x + 2) % 4, (x + 3) % 4

        def stage0(k):
            go(k, yl, x, 0, yn)

        def stage1(k):
            for m, dev in ((1, xp), (2, xm), (3, xo)):
                go(k, yl, x, m, dev)

        def stage2(k):
            have(k, 1 - yl, x, 0)
            for m, dev in ((4, xp), (5, xm), (6, xo)):
                go(k, 1 - yl, x, m, dev)

        def stage4(k):
            for m, a, b in ((1, yl, x3), (2, yl, x1), (3, yl, x2)):
                have(k, a, b, m)
                have(k, 1 - a, b, m + 3)
            ref = buf.at[pl.ds(n * k, n), pl.ds(core * 8, 8)]
            send(ref, ref, sm(k, 7), sib)

        def stage5(k):
            got(buf.at[pl.ds(n * k, n), pl.ds((1 - core) * 8, 8)], sm(k, 7))

        return stage0, stage1, stage2, stage4, stage5

    G0, G1, G2, G4, G5 = gather(gat, gasem, 4)
    N0, N1, N2, N4, N5 = gather(nsb, nssem, NC)
    for k in range(4):
        G0(k)
    G1(0)
    G1(1)
    xh[...] = xhat
    for j in range(NP):
        nrm[j % 8, j // 8] = normed[j].astype(BF16)

    def na_copy(o):
        t = (z + o) % 8
        return rc(
            nrm.at[t], nsb.at[pl.ds(2 * z, 2), sg], (nasem.at[0, o], nasem.at[1, o]),
            (yh * 8 + t, mp),
        )

    def na_send(o, _):
        na_copy(o).start()
        return _

    G2(0)
    G2(1)
    G1(2)
    G2(2)
    lax.fori_loop(1, 8, na_send, 0)
    for i in range(2):
        nsb[2 * z + i, sg] = nrm[z, i]

    def na_wait(o, _):
        s = (z + 8 - o) % 8
        got(nsb.at[pl.ds(2 * s, 2), sg], (nasem.at[0, o], nasem.at[1, o]))
        return _

    lax.fori_loop(1, 16, sg_wait, 0)
    same = [same_image(b) for b in range(2)]
    g = [dot(perm, datt[128 * b : 128 * b + 128, :]).astype(BF16) for b in range(2)]
    G4(0)
    G1(3)
    G2(3)
    G4(1)
    for cp in wcp:
        cp.wait()

    def project(b, n):
        G5(2 * b + n)
        for q in range(2):
            j = 4 * n + 2 * q
            u = [gat[8 * b + j + i].astype(F32) for i in range(2)]
            for m in range(2):
                e = [t[:, 8 * m : 8 * m + 8].reshape(128, PC).astype(BF16) for t in u]
                p = j + 8 * m
                nrow[p, 128 * b : 128 * b + 128] = e[0]
                nrow[p + 1, 128 * b : 128 * b + 128] = e[1]
                lhs = jnp.concatenate(e, axis=1)
                for c in range(3):
                    t = dot(lhs, wv[c, p * PC : (p + 2) * PC, :])
                    proj[c] = t if p == 0 else proj[c] + t

    scale = HD ** (-0.5)

    def z_refs(way, hop, i):
        b, c = CHUNKS[i]
        return zb.at[(z + (8 - hop if way == 0 else hop)) % 8, b, c]

    def z_send(way, hop, i):
        ref = z_refs(way, hop, i)
        send(
            ref, ref, (zsem.at[0, way, hop, i], zsem.at[1, way, hop, i]), zp if way == 0 else zm
        )

    def z_have(way, hop, i):
        got(z_refs(way, hop, i), (zsem.at[0, way, hop - 1, i], zsem.at[1, way, hop - 1, i]))

    def w(hop, i):
        for way in range(2):
            n = hops_of(way, i)
            if hop <= n:
                z_have(way, hop, i)
            if hop < n:
                z_send(way, hop, i)

    def first(i):
        z_send(0, 0, i)
        z_send(1, 0, i)

    def attend(b):
        lanes = [slice(h * HD, (h + 1) * HD) for h in range(2)]
        qkv = [[proj[c, :, lanes[h]].astype(BF16) for c in range(3)] for h in range(2)]
        gh = [g[b][:, lanes[h]] for h in range(2)]
        probs, pb = [], []
        for h in range(2):
            q, k, v = qkv[h]
            s = jnp.where(same[b], dot(q, k, 1, 1) * scale, -1e30)
            e = jnp.exp(s - jnp.max(s, axis=-1, keepdims=True))
            probs.append(e / jnp.sum(e, axis=-1, keepdims=True))
            pb.append(probs[h].astype(BF16))

        def put(i, vals):
            for h in range(2):
                zb[z, b, CHUNKS[i][1], h] = vals[h].astype(BF16)
            if i <= 3:
                first(i)

        put(3 * b, [dot(pb[h], gh[h], 0, 0) for h in range(2)])
        ds = []
        for h in range(2):
            dprob = dot(gh[h], qkv[h][2], 1, 1)
            delta = jnp.sum(probs[h] * dprob, axis=-1, keepdims=True)
            ds.append((probs[h] * (dprob - delta)).astype(BF16))
        put(3 * b + 1, [dot(ds[h], qkv[h][1]) * scale for h in range(2)])
        put(3 * b + 2, [dot(ds[h], qkv[h][0], 0, 0) * scale for h in range(2)])
        outs = [dot(pb[h], qkv[h][2]).astype(BF16) for h in range(2)]
        out = dot(perm_t, jnp.concatenate(outs, axis=1))
        att_o[128 * b : 128 * b + 128, :] = out.astype(BF16)

    project(0, 0)
    project(0, 1)
    attend(0)
    G4(2)
    lax.fori_loop(1, 8, na_wait, 0)
    for k in range(NC):
        N0(k)
    N1(0)
    w(1, 0)
    G4(3)
    N1(1)
    N2(0)
    w(1, 1)
    project(1, 0)
    N2(1)
    w(1, 2)
    project(1, 1)
    w(2, 0)
    w(2, 1)
    attend(1)

    def part(c):
        return jnp.concatenate(
            [jnp.concatenate([zb[z, b, c, 0], zb[z, b, c, 1]], axis=1) for b in range(2)], axis=0
        )

    dq = [part(c) for c in range(3)]

    def dn_step(k):
        def body(j, _):
            at = pl.ds(pl.multiple_of(j * PC, 128), PC)
            t = dot(dq[0], wv[0, at, :], 1, 1)
            t = t + dot(dq[1], wv[1, at, :], 1, 1)
            t = t + dot(dq[2], wv[2, at, :], 1, 1)
            t = t.astype(BF16).astype(F32)
            gp[j] = jnp.sum((t * nrow[j].astype(F32)).reshape(32, 8, PC), axis=0)
            t = t.reshape(2, 16, 8, PC)
            dnb[j] = jnp.concatenate([t[0], t[1]], axis=1).astype(BF16)
            return _

        lax.fori_loop(4 * k, 4 * k + 4, body, 0)
        send(
            dnb.at[pl.ds(4 * k, 4), pl.ds((1 - core) * 8, 8)], rsa.at[pl.ds(4 * k, 4)],
            (rasem.at[0, k], rasem.at[1, k]), sib,
        )

    def s2(k):
        got(rsa.at[pl.ds(4 * k, 4)], (rasem.at[0, k], rasem.at[1, k]))
        for j in range(4 * k, 4 * k + 4):
            mine = dnb[j, pl.ds(core * 8, 8)].astype(F32)
            b1[j] = (mine + rsa[j].astype(F32)).astype(BF16).reshape(2, 4, 16, PC)
        if k < 2:
            send(
                b1.at[pl.ds(4 * k, 4), 1 - yl], rsb.at[pl.ds(4 * k, 4)],
                (rbsem.at[0, k], rbsem.at[1, k]), yn,
            )
        else:
            for o, dev in ((1, xp), (2, xo), (3, xm)):
                send(
                    b1.at[pl.ds(4 * k, 4), :, (x + o) % 4], rsx.at[o - 1, k - 2],
                    (rxsem.at[0, o, k - 2], rxsem.at[1, o, k - 2]), dev,
                )

    def s3(k):
        if k < 2:
            got(rsb.at[pl.ds(4 * k, 4)], (rbsem.at[0, k], rbsem.at[1, k]))
            for j in range(4 * k, 4 * k + 4):
                b2[j] = (b1[j, yl].astype(F32) + rsb[j].astype(F32)).astype(BF16)
            for o, dev in ((1, xp), (2, xo), (3, xm)):
                send(
                    b2.at[pl.ds(4 * k, 4), (x + o) % 4], rsc.at[o - 1, pl.ds(4 * k, 4)],
                    (rcsem.at[0, o, k], rcsem.at[1, o, k]), dev,
                )
        else:
            at = pl.ds(4 * (k - 2), 4)
            for o in range(1, 4):
                got(rsx.at[o - 1, k - 2], (rxsem.at[0, o, k - 2], rxsem.at[1, o, k - 2]))
            for j in range(4):
                t = b1[4 * k + j, :, x].astype(F32)
                for o in range(3):
                    t = t + rsx[o, k - 2, j].astype(F32)
                b3[4 * (k - 2) + j] = t.astype(BF16)
            send(
                b3.at[at, 1 - yl], rsy.at[at], (rysem.at[0, k - 2], rysem.at[1, k - 2]), yn
            )

    def rows_out():
        for k in range(2):
            for o in range(1, 4):
                got(rsc.at[o - 1, pl.ds(4 * k, 4)], (rcsem.at[0, o, k], rcsem.at[1, o, k]))
            got(rsy.at[pl.ds(4 * k, 4)], (rysem.at[0, k], rysem.at[1, k]))
        parts = []
        for j in range(NP):
            if j < 8:
                t = b2[j, x].astype(F32)
                for o in range(3):
                    t = t + rsc[o, j].astype(F32)
            else:
                t = b3[j - 8, yl].astype(F32) + rsy[j - 8].astype(F32)
            parts.append(t * gn[j : j + 1, :])
        m1 = sum(jnp.sum(parts[j], axis=-1, keepdims=True) for j in range(NP)) * (1.0 / D)
        m2 = sum(jnp.sum(parts[j] * xh[j], axis=-1, keepdims=True) for j in range(NP)) * (1.0 / D)
        for j in range(NP):
            t = rstd * (parts[j] - m1 - xh[j] * m2)
            tbg_o[:, j * PC : (j + 1) * PC] = t.astype(BF16)

    kinds = (
        sib, yn, (dp, mpid(yl, x + 1 - 2 * (x % 2), core)), xo,
        (yh * 8 + z + 1 - 2 * (z % 2), mp), (yh * 8 + z + 2 - 4 * ((z // 2) % 2), mp),
        (yh * 8 + (z + 4) % 8, mp), ((1 - yh) * 8 + z, mp),
    )

    def gain(n):
        if n == 0:
            for j in range(NP):
                t = jnp.sum(gp[j], axis=0, keepdims=True)
                for m in range(3):
                    gs[0, 3 * j + m : 3 * j + m + 1, :] = t[:, m * 128 : m * 128 + 128]
        else:
            got(ga.at[n - 1], (gsem.at[0, n - 1], gsem.at[1, n - 1]))
            gs[n] = gs[n - 1] + ga[n - 1]
        if n < 8:
            send(gs.at[n], ga.at[n], (gsem.at[0, n], gsem.at[1, n]), kinds[n])
        else:
            gg_o[...] = gs[n] / gain_ref[...]

    def turn(s, _):
        for i in range(2):
            u = nsb[2 * s + i].astype(F32)
            for b in range(2):
                e = u[:, 8 * b : 8 * b + 8].reshape(128, PC).astype(BF16)
                nt[b, i, :, pl.ds(pl.multiple_of(s * 128, 128), 128)] = e.T
        return _

    def dproj(b, c):
        rhs = jnp.concatenate(
            [jnp.concatenate([zb[s, b, c, 0], zb[s, b, c, 1]], axis=1) for s in range(8)], axis=0
        )
        for i in range(2):
            t = dot(nt[b, i], rhs)
            acc[c, i] = t if b == 0 else acc[c, i] + t

    def swap(c):
        ysnd[c] = acc[c, 1 - yh].astype(BF16)
        send(ysnd.at[c], fin.at[c], (ysem.at[0, c], ysem.at[1, c]), yo)

    def finish(c):
        got(fin.at[c], (ysem.at[0, c], ysem.at[1, c]))
        dproj_o[c] = (acc[c, yh] + fin[c].astype(F32)).astype(BF16)

    w(2, 2)
    dn_step(0)
    w(3, 0)
    dn_step(1)
    s2(0)
    w(3, 1)
    w(1, 3)
    first(4)
    dn_step(2)
    s2(1)
    w(3, 2)
    dn_step(3)
    s2(2)
    w(2, 3)
    w(1, 4)
    first(5)
    gain(0)
    s2(3)
    w(4, 0)
    w(4, 1)
    gain(1)
    w(3, 3)
    w(2, 4)
    w(1, 5)
    for k in range(NC):
        N4(k)
    s3(0)
    gain(2)
    w(4, 2)
    s3(1)
    for k in range(NC):
        N5(k)
    lax.fori_loop(0, 8, turn, 0)
    gain(3)
    dproj(0, 2)
    w(4, 3)
    dproj(1, 2)
    swap(2)
    w(3, 4)
    w(2, 5)
    gain(4)
    s3(2)
    dproj(0, 0)
    w(4, 4)
    dproj(1, 0)
    swap(0)
    w(3, 5)
    gain(5)
    s3(3)
    dproj(0, 1)
    gain(6)
    w(4, 5)
    dproj(1, 1)
    swap(1)
    gain(7)
    finish(2)
    rows_out()
    finish(0)
    gain(8)
    finish(1)

    def drain(i, _):
        r1_copy(i).wait_send()
        sg_copy(i).wait_send()
        r2_copy(i).wait_send()
        return _

    lax.fori_loop(1, 16, drain, 0)

    def drain_na(o, _):
        na_copy(o).wait_send()
        return _

    lax.fori_loop(1, 8, drain_na, 0)
    for item in pend:
        rc(*item).wait_send()


def hand_over(*refs):
    for a, b in zip(refs[:4], refs[4:]):
        b[...] = a[...]


def per_device(tokens, segment_ids, block_order, layer_norm_gain, w_proj, d_attended):
    vm = pl.BlockSpec(memory_space=pltpu.VMEM)
    dma = pltpu.SemaphoreType.DMA
    V = pltpu.VMEM
    big = (NP, 16, 16, PC)
    shapes = (
        jax.ShapeDtypeStruct((256, 256), BF16),
        jax.ShapeDtypeStruct((16, D), BF16),
        jax.ShapeDtypeStruct((3, PC, 256), BF16),
        jax.ShapeDtypeStruct((48, 128), F32),
    )
    made = pl.pallas_call(
        kernel,
        out_shape=shapes,
        in_specs=[
            pl.BlockSpec(memory_space=pltpu.SMEM), vm, vm, vm,
            pl.BlockSpec(memory_space=pl.ANY), vm,
        ],
        out_specs=(vm, vm, vm, vm),
        scratch_shapes=[
            V((3, D, 256), BF16),
            V((NP, 16, PC), BF16),
            V((NP, 16, PC), BF16),
            V((NP, 16, PC), BF16),
            V((8, 128), jnp.int32),
            V((NP, 8, 128), jnp.int32),
            V((NP, PC), F32),
            V((8, 2, 16, PC), BF16),
            V(big, BF16),
            V((NP, 256, PC), BF16),
            V(big, BF16),
            V((NP, 16, PC), F32),
            V((3, 128, 256), F32),
            V((8, 2, 3, 2, 128, HD), BF16),
            V((2, 2, PC, 1024), BF16),
            V(big, BF16),
            V((NP, 8, 16, PC), BF16),
            V((NP, 2, 4, 16, PC), BF16),
            V((8, 4, 16, PC), BF16),
            V((8, 4, 16, PC), BF16),
            V((3, 8, 16, PC), BF16),
            V((3, 2, 4, 2, 16, PC), BF16),
            V((8, 2, 16, PC), BF16),
            V((8, 16, PC), BF16),
            V((3, 2, PC, 256), F32),
            V((3, PC, 256), BF16),
            V((3, PC, 256), BF16),
            V((NP, 8, PC), F32),
            V((9, 48, 128), F32),
            V((8, 48, 128), F32),
            dma((4,)),
            dma((1,)),
            dma((2, 16)),
            dma((2, 16)),
            dma((2, 16)),
            dma((2, 8)),
            dma((2, 4, 8)),
            dma((2, NC, 8)),
            dma((2, 2, 4, 6)),
            dma((2, 4)),
            dma((2, 2)),
            dma((2, 4, 2)),
            dma((2, 4, 2)),
            dma((2, 2)),
            dma((2, 3)),
            dma((2, 8)),
        ],
        compiler_params=pltpu.CompilerParams(
            collective_id=0, has_side_effects=True, vmem_limit_bytes=60 * 1024 * 1024
        ),
    )(
        block_order,
        tokens.reshape(16, D),
        segment_ids,
        layer_norm_gain.reshape(48, 128),
        jnp.transpose(w_proj, (1, 0, 2)),
        d_attended,
    )
    att, tbg, dproj, gg = pl.pallas_call(
        hand_over,
        out_shape=shapes,
        in_specs=[vm] * 4,
        out_specs=(vm,) * 4,
    )(*made)
    return att, tbg.reshape(2, 8, D), jnp.transpose(dproj, (1, 0, 2)), gg.reshape(D)


def solution(mesh):
    placed = (P("dp", "mp", None), P("dp", None), P(), P(), P(None, None, "mp"), P("dp", "mp"))
    return jax.shard_map(
        per_device,
        mesh=mesh,
        in_specs=placed,
        out_specs=(P("dp", "mp"), P("dp", "mp", None), P("dp", None, "mp"), P()),
        check_vma=False,
    )
```

```python
import jax
import jax.numpy as jnp
from jax import lax
from jax.experimental import pallas as pl
from jax.experimental.pallas import tpu as pltpu
from jax.sharding import PartitionSpec as P

D = 6144
HD = 128
PC = 384
NC = 2
NP = 16
F32 = jnp.float32
BF16 = jnp.bfloat16
MESH = pl.DeviceIdType.MESH
CHUNKS = ((0, 2), (0, 0), (0, 1), (1, 2), (1, 0), (1, 1))


def dot(a, b, ca=1, cb=0):
    return lax.dot_general(a, b, (((ca,), (cb,)), ((), ())), preferred_element_type=F32)


def hops_of(way, i):
    return 4 if way == i % 2 else 3


def kernel(
    order, tok, seg, gain_ref, w_hbm, datt,
    att_o, tbg_o, dproj_o, gg_o,
    wv, r1, r2s, r2, segp, sega, gn, nrm, gat, nrow, nsb, xh, proj, zb, nt,
    dnb, rsa, b1, rsb, b2, rsc, rsx, b3, rsy,
    acc, ysnd, fin, gp, gs, ga,
    wsem, lsem, r1sem, r2sem, sgsem, nasem, gasem, nssem, zsem, rasem, rbsem, rcsem, rxsem, rysem, ysem,
    gsem,
):
    dp = lax.axis_index("dp")
    mp = lax.axis_index("mp")
    yh, z = dp // 8, dp % 8
    yl, x, core = mp // 8, (mp // 2) % 4, mp % 2

    def mpid(a, b, c):
        return a * 8 + b * 2 + c

    def mp_of(slot):
        return mpid((slot // 4) % 2, slot % 4, slot // 8)

    sg = core * 8 + yl * 4 + x
    sib = (dp, mpid(yl, x, 1 - core))
    yn = (dp, mpid(1 - yl, x, core))
    xp = (dp, mpid(yl, (x + 1) % 4, core))
    xm = (dp, mpid(yl, (x + 3) % 4, core))
    xo = (dp, mpid(yl, (x + 2) % 4, core))
    zp = (yh * 8 + (z + 1) % 8, mp)
    zm = (yh * 8 + (z + 7) % 8, mp)
    yo = ((1 - yh) * 8 + z, mp)

    def rc(src, dst, sems, dev):
        ss, rs = sems
        return pltpu.make_async_remote_copy(
            src_ref=src, dst_ref=dst, send_sem=ss, recv_sem=rs, device_id=dev, device_id_type=MESH
        )

    def far_first(t):
        half = (t % 8 + 1) // 2
        o = jnp.where(t % 2 == 1, 4 - half, 4 + half) % 8
        return (1 - t // 8) * 8 + o

    def dp_to(i):
        return jnp.where(i >= 8, 1 - yh, yh) * 8 + (z + i) % 8

    def dp_from(i):
        return jnp.where(i >= 8, 1 - yh, yh) * 8 + (z + 16 - i) % 8

    pend = []

    def send(src, dst, sems, dev):
        rc(src, dst, sems, dev).start()
        pend.append((src, dst, sems, dev))

    def got(dst, sems):
        rc(dst, dst, sems, sib).wait_recv()

    wcp = [
        pltpu.make_async_copy(
            w_hbm.at[:, pl.ds(k * 1536, 1536)], wv.at[:, pl.ds(k * 1536, 1536)], wsem.at[k]
        )
        for k in range(4)
    ]
    for cp in wcp:
        cp.start()

    barrier = pltpu.get_barrier_semaphore()

    def greet(t, _):
        pl.semaphore_signal(
            barrier, inc=1, device_id=(dp_to(far_first(t)), mp), device_id_type=MESH
        )
        pl.semaphore_signal(
            barrier, inc=1, device_id=(dp, mp_of((sg + t + 1) % 16)), device_id_type=MESH
        )
        return _

    lax.fori_loop(0, 15, greet, 0)
    segp[...] = jnp.zeros_like(segp)
    segp[0:2, :] = seg[...]
    for j in range(NP):
        gn[j : j + 1, :] = jnp.concatenate(
            [gain_ref[3 * j + n : 3 * j + n + 1, :] for n in range(3)], axis=1
        )
    pl.semaphore_wait(barrier, 30)

    def cols(j):
        return pl.ds(pl.multiple_of(j * PC, 128), PC)

    def r1_copy(i):
        d = dp_to(i)
        return rc(tok.at[:, cols(d)], r1.at[dp], (r1sem.at[0, i], r1sem.at[1, i]), (d, mp))

    def sg_copy(i):
        return rc(segp, sega.at[dp], (sgsem.at[0, i], sgsem.at[1, i]), (dp_to(i), mp))

    def r1_send(t, _):
        r1_copy(far_first(t)).start()
        return _

    lax.fori_loop(0, 15, r1_send, 0)
    own = pltpu.make_async_copy(tok.at[:, cols(dp)], r1.at[dp], lsem.at[0])
    own.start()
    sega[dp] = segp[...]

    def source(i):
        s, r = i >> 3, i & 7
        m = ((s >> 2) & 1) * 8 + (s & 3) * 2 + (s >> 3)
        return m * 8 + r

    ri = lax.broadcasted_iota(jnp.int32, (128, 128), 0)
    ci = lax.broadcasted_iota(jnp.int32, (128, 128), 1)
    perm = jnp.where(source(ri) == ci, 1.0, 0.0).astype(BF16)
    perm_t = jnp.where(source(ci) == ri, 1.0, 0.0).astype(BF16)

    own.wait()

    def r1_wait(i, _):
        got(r1.at[dp_from(i)], (r1sem.at[0, i], r1sem.at[1, i]))
        return _

    lax.fori_loop(1, 16, r1_wait, 0)

    def half_of(p):
        b = order[p]
        t = r1[b >> 1].astype(F32)
        return jnp.where((b & 1) == 1, t[8:16], t[0:8])

    def pick(d):
        return jnp.concatenate([half_of(2 * d), half_of(2 * d + 1)], axis=0).astype(BF16)

    def r2_copy(i):
        d = dp_to(i)
        return rc(r2s.at[d], r2.at[dp], (r2sem.at[0, i], r2sem.at[1, i]), (d, mp))

    def r2_send(t, _):
        i = far_first(t)
        d = dp_to(i)
        r2s[d] = pick(d)
        r2_copy(i).start()
        return _

    lax.fori_loop(0, 15, r2_send, 0)
    r2[dp] = pick(dp)

    def sg_send(i, _):
        sg_copy(i).start()
        return _

    lax.fori_loop(1, 16, sg_send, 0)

    def sg_wait(i, _):
        got(sega.at[dp_from(i)], (sgsem.at[0, i], sgsem.at[1, i]))
        return _

    def ids_of(p):
        b = order[p]
        t = sega[b >> 1].astype(F32)
        return jnp.where((b & 1) == 1, t[1:2], t[0:1])

    def same_image(b):
        ids = jnp.broadcast_to(ids_of(2 * dp + b), (8, 128)).astype(BF16)
        return dot(perm, ids, 1, 1)[:, 0:1] == dot(ids, perm_t)[0:1]

    def r2_wait(i, _):
        got(r2.at[dp_from(i)], (r2sem.at[0, i], r2sem.at[1, i]))
        return _

    lax.fori_loop(1, 16, r2_wait, 0)

    rows = r2[...].astype(F32)
    mean = jnp.sum(jnp.sum(rows, axis=0), axis=-1, keepdims=True) * (1.0 / D)
    cen = rows - mean[None]
    var = jnp.sum(jnp.sum(cen * cen, axis=0), axis=-1, keepdims=True) * (1.0 / D)
    rstd = lax.rsqrt(var + 1e-06)
    xhat = cen * rstd[None]
    normed = [xhat[j] * gn[j : j + 1, :] for j in range(NP)]
    for b in range(2):
        half = slice(8 * b, 8 * b + 8)
        for j in range(8):
            both = jnp.concatenate([normed[j][half], normed[j + 8][half]], axis=0)
            gat[8 * b + j, sg] = both.astype(BF16)

    def gather(buf, sems, chunks):
        n = NP // chunks

        def at(k, slot):
            return buf.at[pl.ds(n * k, n), slot]

        def slot(a, b):
            return core * 8 + a * 4 + b

        def sm(k, m):
            return (sems.at[0, k, m], sems.at[1, k, m])

        def go(k, a, b, m, dev):
            ref = at(k, slot(a, b))
            send(ref, ref, sm(k, m), dev)

        def have(k, a, b, m):
            got(at(k, slot(a, b)), sm(k, m))

        x1, x2, x3 = (x + 1) % 4, (x + 2) % 4, (x + 3) % 4

        def stage0(k):
            go(k, yl, x, 0, yn)

        def stage1(k):
            for m, dev in ((1, xp), (2, xm), (3, xo)):
                go(k, yl, x, m, dev)

        def stage2(k):
            have(k, 1 - yl, x, 0)
            for m, dev in ((4, xp), (5, xm), (6, xo)):
                go(k, 1 - yl, x, m, dev)

        def stage4(k):
            for m, a, b in ((1, yl, x3), (2, yl, x1), (3, yl, x2)):
                have(k, a, b, m)
                have(k, 1 - a, b, m + 3)
            ref = buf.at[pl.ds(n * k, n), pl.ds(core * 8, 8)]
            send(ref, ref, sm(k, 7), sib)

        def stage5(k):
            got(buf.at[pl.ds(n * k, n), pl.ds((1 - core) * 8, 8)], sm(k, 7))

        return stage0, stage1, stage2, stage4, stage5

    G0, G1, G2, G4, G5 = gather(gat, gasem, 4)
    N0, N1, N2, N4, N5 = gather(nsb, nssem, NC)
    for k in range(4):
        G0(k)
    G1(0)
    G1(1)
    xh[...] = xhat
    for j in range(NP):
        nrm[j % 8, j // 8] = normed[j].astype(BF16)

    def na_copy(o):
        t = (z + o) % 8
        return rc(
            nrm.at[t], nsb.at[pl.ds(2 * z, 2), sg], (nasem.at[0, o], nasem.at[1, o]),
            (yh * 8 + t, mp),
        )

    def na_send(o, _):
        na_copy(o).start()
        return _

    G2(0)
    G2(1)
    G1(2)
    G2(2)
    lax.fori_loop(1, 8, na_send, 0)
    for i in range(2):
        nsb[2 * z + i, sg] = nrm[z, i]

    def na_wait(o, _):
        s = (z + 8 - o) % 8
        got(nsb.at[pl.ds(2 * s, 2), sg], (nasem.at[0, o], nasem.at[1, o]))
        return _

    lax.fori_loop(1, 16, sg_wait, 0)
    same = [same_image(b) for b in range(2)]
    g = [dot(perm, datt[128 * b : 128 * b + 128, :]).astype(BF16) for b in range(2)]
    G4(0)
    G1(3)
    G2(3)
    G4(1)
    for cp in wcp:
        cp.wait()

    def project(b, n):
        G5(2 * b + n)
        for q in range(2):
            j = 4 * n + 2 * q
            u = [gat[8 * b + j + i].astype(F32) for i in range(2)]
            for m in range(2):
                e = [t[:, 8 * m : 8 * m + 8].reshape(128, PC).astype(BF16) for t in u]
                p = j + 8 * m
                nrow[p, 128 * b : 128 * b + 128] = e[0]
                nrow[p + 1, 128 * b : 128 * b + 128] = e[1]
                lhs = jnp.concatenate(e, axis=1)
                for c in range(3):
                    t = dot(lhs, wv[c, p * PC : (p + 2) * PC, :])
                    proj[c] = t if p == 0 else proj[c] + t

    scale = HD ** (-0.5)

    def z_refs(way, hop, i):
        b, c = CHUNKS[i]
        return zb.at[(z + (8 - hop if way == 0 else hop)) % 8, b, c]

    def z_send(way, hop, i):
        ref = z_refs(way, hop, i)
        send(
            ref, ref, (zsem.at[0, way, hop, i], zsem.at[1, way, hop, i]), zp if way == 0 else zm
        )

    def z_have(way, hop, i):
        got(z_refs(way, hop, i), (zsem.at[0, way, hop - 1, i], zsem.at[1, way, hop - 1, i]))

    def w(hop, i):
        for way in range(2):
            n = hops_of(way, i)
            if hop <= n:
                z_have(way, hop, i)
            if hop < n:
                z_send(way, hop, i)

    def first(i):
        z_send(0, 0, i)
        z_send(1, 0, i)

    def attend(b):
        lanes = [slice(h * HD, (h + 1) * HD) for h in range(2)]
        qkv = [[proj[c, :, lanes[h]].astype(BF16) for c in range(3)] for h in range(2)]
        gh = [g[b][:, lanes[h]] for h in range(2)]
        probs, pb = [], []
        for h in range(2):
            q, k, v = qkv[h]
            s = jnp.where(same[b], dot(q, k, 1, 1) * scale, -1e30)
            e = jnp.exp(s - jnp.max(s, axis=-1, keepdims=True))
            probs.append(e / jnp.sum(e, axis=-1, keepdims=True))
            pb.append(probs[h].astype(BF16))

        def put(i, vals):
            for h in range(2):
                zb[z, b, CHUNKS[i][1], h] = vals[h].astype(BF16)
            if i <= 4:
                first(i)

        put(3 * b, [dot(pb[h], gh[h], 0, 0) for h in range(2)])
        ds = []
        for h in range(2):
            dprob = dot(gh[h], qkv[h][2], 1, 1)
            delta = jnp.sum(probs[h] * dprob, axis=-1, keepdims=True)
            ds.append((probs[h] * (dprob - delta)).astype(BF16))
        put(3 * b + 1, [dot(ds[h], qkv[h][1]) * scale for h in range(2)])
        put(3 * b + 2, [dot(ds[h], qkv[h][0], 0, 0) * scale for h in range(2)])
        outs = [dot(pb[h], qkv[h][2]).astype(BF16) for h in range(2)]
        out = dot(perm_t, jnp.concatenate(outs, axis=1))
        att_o[128 * b : 128 * b + 128, :] = out.astype(BF16)

    project(0, 0)
    project(0, 1)
    attend(0)
    G4(2)
    lax.fori_loop(1, 8, na_wait, 0)
    for k in range(NC):
        N0(k)
    N1(0)
    project(1, 0)
    w(1, 0)
    G4(3)
    N1(1)
    N2(0)
    w(1, 1)
    N2(1)
    w(1, 2)
    project(1, 1)
    w(2, 0)
    w(2, 1)
    attend(1)

    def part(c):
        return jnp.concatenate(
            [jnp.concatenate([zb[z, b, c, 0], zb[z, b, c, 1]], axis=1) for b in range(2)], axis=0
        )

    dq = [part(c) for c in range(3)]

    def dn_step(k):
        def body(j, _):
            at = pl.ds(pl.multiple_of(j * PC, 128), PC)
            t = dot(dq[0], wv[0, at, :], 1, 1)
            t = t + dot(dq[1], wv[1, at, :], 1, 1)
            t = t + dot(dq[2], wv[2, at, :], 1, 1)
            t = t.astype(BF16).astype(F32)
            gp[j] = jnp.sum((t * nrow[j].astype(F32)).reshape(32, 8, PC), axis=0)
            t = t.reshape(2, 16, 8, PC)
            dnb[j] = jnp.concatenate([t[0], t[1]], axis=1).astype(BF16)
            return _

        lax.fori_loop(4 * k, 4 * k + 4, body, 0)
        send(
            dnb.at[pl.ds(4 * k, 4), pl.ds((1 - core) * 8, 8)], rsa.at[pl.ds(4 * k, 4)],
            (rasem.at[0, k], rasem.at[1, k]), sib,
        )

    def s2(k):
        got(rsa.at[pl.ds(4 * k, 4)], (rasem.at[0, k], rasem.at[1, k]))
        for j in range(4 * k, 4 * k + 4):
            mine = dnb[j, pl.ds(core * 8, 8)].astype(F32)
            b1[j] = (mine + rsa[j].astype(F32)).astype(BF16).reshape(2, 4, 16, PC)
        if k < 2:
            send(
                b1.at[pl.ds(4 * k, 4), 1 - yl], rsb.at[pl.ds(4 * k, 4)],
                (rbsem.at[0, k], rbsem.at[1, k]), yn,
            )
        else:
            for o, dev in ((1, xp), (2, xo), (3, xm)):
                send(
                    b1.at[pl.ds(4 * k, 4), :, (x + o) % 4], rsx.at[o - 1, k - 2],
                    (rxsem.at[0, o, k - 2], rxsem.at[1, o, k - 2]), dev,
                )

    def s3(k):
        if k < 2:
            got(rsb.at[pl.ds(4 * k, 4)], (rbsem.at[0, k], rbsem.at[1, k]))
            for j in range(4 * k, 4 * k + 4):
                b2[j] = (b1[j, yl].astype(F32) + rsb[j].astype(F32)).astype(BF16)
            for o, dev in ((1, xp), (2, xo), (3, xm)):
                send(
                    b2.at[pl.ds(4 * k, 4), (x + o) % 4], rsc.at[o - 1, pl.ds(4 * k, 4)],
                    (rcsem.at[0, o, k], rcsem.at[1, o, k]), dev,
                )
        else:
            at = pl.ds(4 * (k - 2), 4)
            for o in range(1, 4):
                got(rsx.at[o - 1, k - 2], (rxsem.at[0, o, k - 2], rxsem.at[1, o, k - 2]))
            for j in range(4):
                t = b1[4 * k + j, :, x].astype(F32)
                for o in range(3):
                    t = t + rsx[o, k - 2, j].astype(F32)
                b3[4 * (k - 2) + j] = t.astype(BF16)
            send(
                b3.at[at, 1 - yl], rsy.at[at], (rysem.at[0, k - 2], rysem.at[1, k - 2]), yn
            )

    def rows_out():
        for k in range(2):
            for o in range(1, 4):
                got(rsc.at[o - 1, pl.ds(4 * k, 4)], (rcsem.at[0, o, k], rcsem.at[1, o, k]))
            got(rsy.at[pl.ds(4 * k, 4)], (rysem.at[0, k], rysem.at[1, k]))
        parts = []
        for j in range(NP):
            if j < 8:
                t = b2[j, x].astype(F32)
                for o in range(3):
                    t = t + rsc[o, j].astype(F32)
            else:
                t = b3[j - 8, yl].astype(F32) + rsy[j - 8].astype(F32)
            parts.append(t * gn[j : j + 1, :])
        m1 = sum(jnp.sum(parts[j], axis=-1, keepdims=True) for j in range(NP)) * (1.0 / D)
        m2 = sum(jnp.sum(parts[j] * xh[j], axis=-1, keepdims=True) for j in range(NP)) * (1.0 / D)
        for j in range(NP):
            t = rstd * (parts[j] - m1 - xh[j] * m2)
            tbg_o[:, j * PC : (j + 1) * PC] = t.astype(BF16)

    zl, hi = z % 4, yh * 2 + z // 4

    def hi_dev(n):
        return ((n // 2) * 8 + (n % 2) * 4 + zl, mp)

    kinds = (
        (2, core, lambda n: (dp, mpid(yl, x, n))),
        (4, zl, lambda n: (yh * 8 + z - zl + n, mp)),
        (4, hi, hi_dev),
        (4, x, lambda n: (dp, mpid(yl, n, core))),
        (2, yl, lambda n: (dp, mpid(n, x, core))),
    )

    def gain(n):
        if n == 0:
            for j in range(NP):
                t = jnp.sum(gp[j], axis=0, keepdims=True)
                for m in range(3):
                    gs[0, 3 * j + m : 3 * j + m + 1, :] = t[:, m * 128 : m * 128 + 128]
        else:
            size, rank, _ = kinds[n - 1]
            ga[n - 1, rank] = gs[n - 1]
            for o in range(1, size):
                got(ga.at[n - 1, (rank + size - o) % size], (gsem.at[0, n - 1, o], gsem.at[1, n - 1, o]))
            t = ga[n - 1, 0] + ga[n - 1, 1]
            if size == 4:
                t = t + ga[n - 1, 2] + ga[n - 1, 3]
            gs[n] = t
        if n < 5:
            size, rank, dev = kinds[n]
            for o in range(1, size):
                send(
                    gs.at[n], ga.at[n, rank], (gsem.at[0, n, o], gsem.at[1, n, o]),
                    dev((rank + o) % size),
                )
        else:
            gg_o[...] = gs[n] / gain_ref[...]

    def turn(s, _):
        for i in range(2):
            u = nsb[2 * s + i].astype(F32)
            for b in range(2):
                e = u[:, 8 * b : 8 * b + 8].reshape(128, PC).astype(BF16)
                nt[b, i, :, pl.ds(pl.multiple_of(s * 128, 128), 128)] = e.T
        return _

    def dproj(b, c):
        rhs = jnp.concatenate(
            [jnp.concatenate([zb[s, b, c, 0], zb[s, b, c, 1]], axis=1) for s in range(8)], axis=0
        )
        for i in range(2):
            t = dot(nt[b, i], rhs)
            acc[c, i] = t if b == 0 else acc[c, i] + t

    def swap(c):
        ysnd[c] = acc[c, 1 - yh].astype(BF16)
        send(ysnd.at[c], fin.at[c], (ysem.at[0, c], ysem.at[1, c]), yo)

    def finish(c):
        got(fin.at[c], (ysem.at[0, c], ysem.at[1, c]))
        dproj_o[c] = (acc[c, yh] + fin[c].astype(F32)).astype(BF16)

    w(2, 2)
    dn_step(0)
    w(3, 0)
    dn_step(1)
    s2(0)
    w(3, 1)
    w(1, 3)
    first(5)
    dn_step(2)
    s2(1)
    w(3, 2)
    w(1, 4)
    dn_step(3)
    gain(0)
    s2(2)
    w(2, 3)
    gain(1)
    s2(3)
    w(4, 0)
    w(4, 1)
    for k in range(NC):
        N4(k)
    w(1, 5)
    s3(0)
    w(2, 4)
    for k in range(NC):
        N5(k)
    lax.fori_loop(0, 4, turn, 0)
    w(3, 3)
    gain(2)
    s3(1)
    lax.fori_loop(4, 8, turn, 0)
    w(2, 5)
    dproj(0, 2)
    w(4, 2)
    w(3, 4)
    w(4, 3)
    dproj(1, 2)
    swap(2)
    s3(2)
    gain(3)
    w(3, 5)
    dproj(0, 0)
    w(4, 4)
    dproj(1, 0)
    swap(0)
    s3(3)
    dproj(0, 1)
    gain(4)
    w(4, 5)
    dproj(1, 1)
    swap(1)
    rows_out()

    def drain(i, _):
        r1_copy(i).wait_send()
        sg_copy(i).wait_send()
        r2_copy(i).wait_send()
        return _

    lax.fori_loop(1, 16, drain, 0)

    def drain_na(o, _):
        na_copy(o).wait_send()
        return _

    lax.fori_loop(1, 8, drain_na, 0)
    for item in pend[:-3]:
        rc(*item).wait_send()
    finish(2)
    finish(0)
    gain(5)
    finish(1)
    for item in pend[-3:]:
        rc(*item).wait_send()


def hand_over(*refs):
    for a, b in zip(refs[:4], refs[4:]):
        b[...] = a[...]


def per_device(tokens, segment_ids, block_order, layer_norm_gain, w_proj, d_attended):
    vm = pl.BlockSpec(memory_space=pltpu.VMEM)
    dma = pltpu.SemaphoreType.DMA
    V = pltpu.VMEM
    big = (NP, 16, 16, PC)
    shapes = (
        jax.ShapeDtypeStruct((256, 256), BF16),
        jax.ShapeDtypeStruct((16, D), BF16),
        jax.ShapeDtypeStruct((3, PC, 256), BF16),
        jax.ShapeDtypeStruct((48, 128), F32),
    )
    made = pl.pallas_call(
        kernel,
        out_shape=shapes,
        in_specs=[
            pl.BlockSpec(memory_space=pltpu.SMEM), vm, vm, vm,
            pl.BlockSpec(memory_space=pl.ANY), vm,
        ],
        out_specs=(vm, vm, vm, vm),
        scratch_shapes=[
            V((3, D, 256), BF16),
            V((NP, 16, PC), BF16),
            V((NP, 16, PC), BF16),
            V((NP, 16, PC), BF16),
            V((8, 128), jnp.int32),
            V((NP, 8, 128), jnp.int32),
            V((NP, PC), F32),
            V((8, 2, 16, PC), BF16),
            V(big, BF16),
            V((NP, 256, PC), BF16),
            V(big, BF16),
            V((NP, 16, PC), F32),
            V((3, 128, 256), F32),
            V((8, 2, 3, 2, 128, HD), BF16),
            V((2, 2, PC, 1024), BF16),
            V(big, BF16),
            V((NP, 8, 16, PC), BF16),
            V((NP, 2, 4, 16, PC), BF16),
            V((8, 4, 16, PC), BF16),
            V((8, 4, 16, PC), BF16),
            V((3, 8, 16, PC), BF16),
            V((3, 2, 4, 2, 16, PC), BF16),
            V((8, 2, 16, PC), BF16),
            V((8, 16, PC), BF16),
            V((3, 2, PC, 256), F32),
            V((3, PC, 256), BF16),
            V((3, PC, 256), BF16),
            V((NP, 8, PC), F32),
            V((6, 48, 128), F32),
            V((5, 4, 48, 128), F32),
            dma((4,)),
            dma((1,)),
            dma((2, 16)),
            dma((2, 16)),
            dma((2, 16)),
            dma((2, 8)),
            dma((2, 4, 8)),
            dma((2, NC, 8)),
            dma((2, 2, 4, 6)),
            dma((2, 4)),
            dma((2, 2)),
            dma((2, 4, 2)),
            dma((2, 4, 2)),
            dma((2, 2)),
            dma((2, 3)),
            dma((2, 5, 4)),
        ],
        compiler_params=pltpu.CompilerParams(
            collective_id=0, has_side_effects=True, vmem_limit_bytes=60 * 1024 * 1024
        ),
    )(
        block_order,
        tokens.reshape(16, D),
        segment_ids,
        layer_norm_gain.reshape(48, 128),
        jnp.transpose(w_proj, (1, 0, 2)),
        d_attended,
    )
    att, tbg, dproj, gg = pl.pallas_call(
        hand_over,
        out_shape=shapes,
        in_specs=[vm] * 4,
        out_specs=(vm,) * 4,
    )(*made)
    return att, tbg.reshape(2, 8, D), jnp.transpose(dproj, (1, 0, 2)), gg.reshape(D)


def solution(mesh):
    placed = (P("dp", "mp", None), P("dp", None), P(), P(), P(None, None, "mp"), P("dp", "mp"))
    return jax.shard_map(
        per_device,
        mesh=mesh,
        in_specs=placed,
        out_specs=(P("dp", "mp"), P("dp", "mp", None), P("dp", None, "mp"), P()),
        check_vma=False,
    )
```
